32 devices in a mesh: groups: 2 (over x), col: 16 (over z, y, core).
Axes of the slice: x: 2, y: 2, z: 4, core: 2. Of those that a mesh axis runs over, the one named last changes fastest.
Arguments:
- tokens: bfloat16 [4096, 4096], P(('groups', 'col')), parts along dimension 0, may hold values from -6 to 6
- weight_in: bfloat16 [4096, 1024], P('col'), may hold values from -0.09375 to 0.09375
- weight_out: bfloat16 [1024, 4096], P(None, 'col'), may hold values from -0.1875 to 0.1875
- up_quant: bfloat16 [16, 1024, 2688], P('col'), may hold values from -4 to 4
- up_scale: float32 [16, 8, 21], P('col'), may hold values from 0.0156 to 0.0625
- down_quant: bfloat16 [16, 2688, 1024], P('col'), may hold values from -4 to 4
- down_scale: float32 [16, 21, 8], P('col'), may hold values from 0.0097 to 0.0386
- routing: int32 [4096, 4], P(('groups', 'col')), parts along dimension 0, may hold values from 0 to 15, all different within a row; in each aligned block of 128 rows (0 to 127, 128 to 255, ...) at most 48 rows name the same one
- gate_weights: float32 [4096, 4], P(('groups', 'col')), parts along dimension 0, may hold values from 0.1 to 1
Outputs:
- mixed: bfloat16 [4096, 4096], P(('groups', 'col')), parts along dimension 0
The draws below stay inside these ranges and needn't reach their ends.
There are 2 independent parts, one for each index of `groups`. The reference program is written for one: setup_inputs(seed, part) draws one part's arguments, and reference() takes and returns one part's arrays. A program takes and returns all parts, laid end to end along the dimension named above; an argument that names none is the same for every part. Nothing has to cross between parts.
Inputs may be any that keep to these rules, and one draw needn't show every extreme that they name: `routing`: each row names 4 different experts. Within the 128 rows of one index of col (aligned blocks) no expert is named more than 48 times, a bound that some block reaches.
All inputs are finite; a program needn't handle non-finite values.
Results may differ from the reference program's by a relative error of at most 0.0084.
Values may be sent and summed in bfloat16 or wider, within the bound.
A program may use at most 128 MiB of HBM per device.

```python
import math
import jax
import jax.numpy as jnp
import numpy as np
from jax import lax

D = 4096
L = 1024
H = 2688
QB = 128
TOK_DEV = 128
TOP = 4
EXPERTS = 16
CAP = 48
TOKENS = 2048
N_COL = 16


def block_levels(key, extent, cuts, low, largest):
    factor_of, own = 1.0, jax.random.fold_in(key, 6)
    for position, parts in cuts:
        draws = jnp.exp(jax.random.uniform(jax.random.fold_in(own, position), (parts,), jnp.float32, low / len(cuts), largest / len(cuts)))
        factor_of = factor_of * jnp.repeat(draws, extent[position] // parts).reshape([-1 if axis == position else 1 for axis in range(len(extent))])
    return factor_of


def shared_out(own_key, own, number, rows, number_of, top, reach, lean):
    order = jax.random.permutation(own_key, number_of)
    packed, usual = load_shares(number_of, rows * top, reach, lean, True), load_shares(number_of, rows * top, reach, lean, False)
    places = jnp.arange(number_of)

    def named(tallies, turn):
        used = int((tallies > 0).sum())
        fixed = max(1, used // 4)
        moved = fixed + (places - fixed + turn * (used - fixed)) % max(1, number_of - fixed)
        return jnp.zeros((number_of,), jnp.int32).at[order[jnp.where(places < fixed, places, moved)]].set(jnp.asarray(tallies, jnp.int32))

    tallies = jnp.where(number % 4 == 0, named(packed, number // 4), named(usual, number - number // 4 - 1))
    mixed = jax.random.permutation(jax.random.fold_in(own, 3), number_of)
    source_of, sink = mixed[0:number_of // 2 * 2:2], mixed[1:number_of // 2 * 2:2]
    room = jnp.minimum(tallies[source_of] - 1, reach - tallies[sink]) // 2
    room = jnp.where((source_of == order[0]) | (sink == order[0]) | (tallies[sink] == 0), 0, jnp.maximum(room, 0))
    moved = jax.random.randint(jax.random.fold_in(own, 4), (number_of // 2,), 0, 1 << 20) % (room + 1)
    tallies = tallies.at[source_of].add(-moved).at[sink].add(moved)
    members = jnp.searchsorted(jnp.cumsum(tallies), jnp.arange(rows * top), side="right").astype(jnp.int32)
    grid = members.reshape(top, rows).T
    grid = grid[jax.random.permutation(jax.random.fold_in(own, 1), rows)]
    turn = jax.random.randint(jax.random.fold_in(own, 2), (rows, 1), 0, top)
    return jnp.take_along_axis(grid, (jnp.arange(top)[None, :] + turn) % top, axis=1)


def load_shares(number_of, total, limit, slope, full):
    loads = [(1 << 20) // math.isqrt(standing ** slope) + 1 for standing in range(1, number_of + 1)]
    largest = limit if full else min(limit, max(-(-total // number_of), total * loads[0] // sum(loads)))
    least = 1 if total - largest >= number_of - 1 else 0
    given, spare = [largest] + [least] * (number_of - 1), total - largest - least * (number_of - 1)
    while spare > 0:
        movable = [i for i in range(1, number_of) if given[i] < largest] or [i for i in range(1, number_of) if given[i] < limit]
        whole, remaining = sum([loads[i] for i in movable]), spare
        for i in movable:
            addition = min(limit - given[i], max(1, remaining * loads[i] // whole), spare)
            given[i] = given[i] + addition
            spare = spare - addition
    return np.array(given)


def noise(own_key, shape, scale, reach, pieces=(), held_as=jnp.bfloat16):
    entries = scale * jax.random.normal(own_key, shape, jnp.float32)
    if pieces:
        entries = entries * block_levels(own_key, shape, pieces, -0.22, 0.18)
    return jnp.clip(entries, -reach, reach).astype(held_as)


def setup_inputs(seed: int = 0, part: int = 0) -> dict:
    keys = jax.random.split(jax.random.key(seed), 10)
    own_keys = jax.random.split(jax.random.fold_in(keys[9], part), 10)
    tokens = noise(own_keys[0], (TOKENS, D), 1.0, 6.0, ((0, 16),))
    weight_in = noise(keys[1], (D, L), D ** -0.5, 0.09375, ((0, 16),))
    weight_out = noise(keys[2], (L, D), L ** -0.5, 0.1875, ((1, 16),))
    up_quant = noise(keys[3], (EXPERTS, L, H), 1.0, 4.0, ((0, 16),))
    up_scale = jnp.clip(jnp.exp(math.log(0.0625) - 1.3878957 * jax.random.uniform(keys[4], (EXPERTS, L // QB, H // QB), jnp.float32) ** block_levels(keys[4], (EXPERTS, L // QB, H // QB), ((0, 16),), -0.2, 0.2)), 0.0156, 0.0625)
    down_quant = noise(keys[5], (EXPERTS, H, L), 1.0, 4.0, ((0, 16),))
    down_scale = jnp.clip(jnp.exp(math.log(0.0386) - 1.3811264 * jax.random.uniform(keys[6], (EXPERTS, H // QB, L // QB), jnp.float32) ** block_levels(keys[6], (EXPERTS, H // QB, L // QB), ((0, 16),), -0.2, 0.2)), 0.0097, 0.0386)
    routing_keys = jax.random.split(jax.random.fold_in(own_keys[7], 1), TOKENS // TOK_DEV)
    routing_turns = jax.random.permutation(jax.random.fold_in(own_keys[7], 3), TOKENS // TOK_DEV)
    routing = jax.vmap(lambda own, number: shared_out(jax.random.fold_in(own_keys[7], 2), own, number, TOK_DEV, EXPERTS, TOP, CAP, 0))(routing_keys, routing_turns).reshape((TOKENS, TOP))
    gate_weights = jnp.clip(0.1 + 0.9 * jax.random.uniform(own_keys[8], (TOKENS, TOP), jnp.float32) ** block_levels(own_keys[8], (TOKENS, TOP), ((0, 16),), -0.2, 0.2), 0.1, 1.0)
    return {"tokens": tokens, "weight_in": weight_in, "weight_out": weight_out, "up_quant": up_quant, "up_scale": up_scale, "down_quant": down_quant, "down_scale": down_scale, "routing": routing, "gate_weights": gate_weights}


def dequant(quant, scale):
    expanded = jnp.repeat(jnp.repeat(scale, QB, axis=-2), QB, axis=-1)
    return (quant.astype(jnp.float32) * expanded).astype(jnp.bfloat16)


def reference(tokens, weight_in, weight_out, up_quant, up_scale, down_quant, down_scale, routing, gate_weights):
    latent = jnp.dot(tokens, weight_in, preferred_element_type=jnp.float32).astype(jnp.bfloat16)
    flat = routing.reshape(-1).astype(jnp.int32)
    onehot = (flat[:, None] == jnp.arange(EXPERTS, dtype=jnp.int32)[None, :]).astype(jnp.int32)
    before = jnp.cumsum(onehot, axis=0) - onehot
    rank = jnp.sum(before * onehot, axis=1).astype(jnp.int32)
    token_of = (jnp.arange(TOKENS * TOP, dtype=jnp.int32) // TOP).astype(jnp.int32)
    table = jnp.zeros((EXPERTS, N_COL * CAP), jnp.int32).at[flat, rank].set(token_of)

    def expert(operands):
        rows_index, uq, us, dq, ds = operands
        up_w = dequant(uq, us)
        down_w = dequant(dq, ds)
        inputs = latent[rows_index]
        hidden = jnp.dot(inputs, up_w, preferred_element_type=jnp.float32)
        act = jnp.square(jax.nn.relu(hidden)).astype(jnp.bfloat16)
        return jnp.dot(act, down_w, preferred_element_type=jnp.float32).astype(jnp.bfloat16)

    outputs = lax.map(expert, (table, up_quant, up_scale, down_quant, down_scale))
    picked = outputs[flat, rank].reshape(TOKENS, TOP, L).astype(jnp.float32)
    combined = jnp.sum(picked * gate_weights[:, :, None], axis=1).astype(jnp.bfloat16)
    return jnp.dot(combined, weight_out, preferred_element_type=jnp.float32).astype(jnp.bfloat16)
```

```python
import functools

import jax
import jax.numpy as jnp
from jax import lax
from jax.experimental import pallas as pl
from jax.experimental.pallas import tpu as pltpu
from jax.sharding import PartitionSpec as P

QUAD = 4
CHUNK = 4
MESH = pl.DeviceIdType.MESH
F32, BF16 = jnp.float32, jnp.bfloat16


def dequant(quant, scale):
    block = quant.shape[1] // scale.shape[1]
    expanded = jnp.repeat(jnp.repeat(scale, block, axis=-2), block, axis=-1)
    return (quant.astype(F32) * expanded).astype(BF16)


def capacity_of(tok_rows, top_count, experts):
    return max(2, 3 * tok_rows * top_count // (2 * experts))


def plain_body(
    tokens, weight_in, weight_out, up_quant, up_scale, down_quant, down_scale, routing, gate_weights
):
    tok_rows, top_count = routing.shape
    exp_local = up_quant.shape[0]
    n_devices = lax.axis_size("col")
    experts = exp_local * n_devices
    capacity = capacity_of(tok_rows, top_count, experts)
    width = weight_in.shape[1]
    slots_all = experts * capacity
    latent = jnp.dot(
        tokens,
        lax.all_gather(weight_in, "col", axis=0, tiled=True),
        preferred_element_type=F32,
    ).astype(BF16)
    flat = routing.reshape(-1)
    onehot = (flat[:, None] == jnp.arange(experts, dtype=jnp.int32)[None, :]).astype(BF16)
    places = jnp.arange(flat.shape[0], dtype=jnp.int32)
    earlier = (places[:, None] > places[None, :]).astype(BF16)
    before = jnp.dot(earlier, onehot, preferred_element_type=F32)
    slot_rank = jnp.sum(before * onehot.astype(F32), axis=1).astype(jnp.int32)
    target = flat * capacity + slot_rank
    hits = (target[:, None] == jnp.arange(slots_all, dtype=jnp.int32)[None, :]).astype(BF16)
    hits = jnp.sum(hits.reshape(tok_rows, top_count, slots_all), axis=1)
    outgoing = jnp.einsum("tr,tl->rl", hits, latent, preferred_element_type=F32).astype(BF16)
    outgoing = outgoing.reshape(n_devices, exp_local, capacity, width)
    up_w = dequant(up_quant, up_scale)
    down_w = dequant(down_quant, down_scale)
    piece = lax.all_to_all(outgoing, "col", split_axis=0, concat_axis=0, tiled=True)
    sources, local_count, count, lanes = piece.shape
    rows = piece.transpose(1, 0, 2, 3).reshape(local_count, sources * count, lanes)
    hidden = jnp.einsum("erl,elh->erh", rows, up_w, preferred_element_type=F32)
    act = jnp.square(jax.nn.relu(hidden)).astype(BF16)
    result = jnp.einsum("erh,ehl->erl", act, down_w, preferred_element_type=F32).astype(BF16)
    computed = result.reshape(local_count, sources, count, lanes).transpose(1, 0, 2, 3)
    returned = lax.all_to_all(computed, "col", split_axis=0, concat_axis=0, tiled=True)
    back_rows = returned.reshape(slots_all, width)
    picked = back_rows[target].reshape(tok_rows, top_count, width).astype(F32)
    combined = jnp.sum(picked * gate_weights[:, :, None], axis=1).astype(BF16)
    mixed = jnp.dot(
        combined,
        lax.all_gather(weight_out, "col", axis=1, tiled=True),
        preferred_element_type=F32,
    )
    return mixed.astype(BF16)


def layer_kernel(
    n, n_groups, cap,
    tokens, w_in, w_out, upq, ups, dnq, dns, routing, gates,
    out,
    win, tq, tr, ps, pr, lat, hits, ghi, glo, disp, rows_in, res, back, upw, dnw, act, wl, comb, cr,
    sb, out_v,
    s_local, s_tq, s_win, r_win, s_winx, r_winx, s_tok, r_tok, s_par, r_par, s_disp, r_disp, s_ret, r_ret,
    s_wo, r_wo, s_woy, r_woy, s_wox, r_wox, s_comb, r_comb, s_out, r_out,
):
    lines = n // QUAD
    half = QUAD // 2
    toks = tokens.shape[0]
    kd, wide = w_in.shape
    wd = w_out.shape[1]
    hid = upw.shape[1]
    top = routing.shape[1]
    slots = n * cap
    me, grp = lax.axis_index("col"), lax.axis_index("groups")
    z, q = me // QUAD, lax.rem(me, QUAD)

    def at(col):
        return (grp, col)

    def across(step):
        return (lax.rem(grp + step, n_groups), me)

    def remote(src, dst, send, recv, to):
        return pltpu.make_async_remote_copy(
            src_ref=src, dst_ref=dst, send_sem=send, recv_sem=recv, device_id=to, device_id_type=MESH
        )

    tok_loads = []
    for i in range(n):
        line, lane = i // QUAD, i % QUAD
        tok_loads.append(
            pltpu.make_async_copy(
                tokens.at[:, pl.ds(i * kd, kd)], tq.at[lane, :, pl.ds(line * kd, kd)], s_tq.at[i]
            )
        )
    my_rows = pl.ds(pl.multiple_of(z * kd, kd), kd)
    loads = [
        pltpu.make_async_copy(w_in, win.at[my_rows], s_local.at[0]),
        pltpu.make_async_copy(upq, upw, s_local.at[1]),
        pltpu.make_async_copy(dnq, dnw, s_local.at[2]),
        pltpu.make_async_copy(w_out, wl.at[0, z], s_local.at[3]),
    ]
    for c in tok_loads:
        c.start()
    for c in loads:
        c.start()

    barrier = pltpu.get_barrier_semaphore()
    for d in range(1, n):
        pl.semaphore_signal(barrier, inc=1, device_id=at(lax.rem(me + d, n)), device_id_type=MESH)
    for d in range(1, n_groups):
        pl.semaphore_signal(barrier, inc=1, device_id=across(d), device_id_type=MESH)
    pl.semaphore_wait(barrier, n - 1 + n_groups - 1)

    kp = kd // n_groups
    win_sends = []
    for d in range(1, lines):
        src = w_in.at[pl.ds(pl.multiple_of(grp * kp, kp), kp)]
        dst = win.at[pl.ds(pl.multiple_of(z * kd + grp * kp, kp), kp)]
        c = remote(src, dst, s_win.at[d - 1], r_win.at[d - 1], at(lax.rem(z + d, lines) * QUAD + q))
        c.start()
        win_sends.append(c)
    for c in tok_loads:
        c.wait()
    tok_sends = []
    for d in range(1, QUAD):
        to = lax.rem(q + d, QUAD)
        c = remote(tq.at[to], tr.at[d - 1], s_tok.at[d - 1], r_tok.at[d - 1], at(z * QUAD + to))
        c.start()
        tok_sends.append(c)

    lane_e = lax.broadcasted_iota(jnp.int32, (toks, n), 1)
    mask = jnp.zeros((toks, n), F32)
    gate = jnp.zeros((toks, n), F32)
    for k in range(top):
        eq = (routing[:, k : k + 1] == lane_e).astype(F32)
        mask = mask + eq
        gate = gate + eq * gates[:, k : k + 1]
    earlier = (
        lax.broadcasted_iota(jnp.int32, (toks, toks), 0) > lax.broadcasted_iota(jnp.int32, (toks, toks), 1)
    ).astype(F32).astype(BF16)
    rank = jnp.dot(earlier, mask.astype(BF16), preferred_element_type=F32)
    out_of_range = -float(1 << slots.bit_length())
    rank = jnp.where(mask > 0.5, rank, out_of_range).astype(BF16)
    row = lax.broadcasted_iota(jnp.int32, (n, slots), 0)
    col = lax.broadcasted_iota(jnp.int32, (n, slots), 1)
    inside = ((col >= row * cap) & (col < row * cap + cap)).astype(F32)
    start = jnp.sum(inside * (row * cap).astype(F32), axis=0, keepdims=True)
    spread = inside.astype(BF16)
    rank_x = jnp.dot(rank, spread, preferred_element_type=F32)
    slot = lax.broadcasted_iota(jnp.int32, (toks, slots), 1).astype(F32)
    hit = (rank_x + start == slot).astype(F32)
    hits[...] = hit.astype(BF16)
    gate_hi = gate.astype(BF16)
    gate_lo = (gate - gate_hi.astype(F32)).astype(BF16)
    ghi[...] = (hit * jnp.dot(gate_hi, spread, preferred_element_type=F32)).astype(BF16)
    glo[...] = (hit * jnp.dot(gate_lo, spread, preferred_element_type=F32)).astype(BF16)

    def expand(weights, scales):
        rows_n, cols_n = scales.shape
        br, bc = weights.shape[0] // rows_n, weights.shape[1] // cols_n

        def step(i, carry):
            rows = pl.ds(pl.multiple_of(i * br, br), br)
            for j in range(cols_n):
                cols = slice(j * bc, (j + 1) * bc)
                weights[rows, cols] = (weights[rows, cols].astype(F32) * scales[i, j]).astype(BF16)
            return carry

        lax.fori_loop(0, rows_n, step, 0)

    loads[1].wait()
    expand(upw, ups)

    winx_sends = []
    for d in range(1, lines):
        win_sends[d - 1].wait_recv()
        src = win.at[pl.ds(pl.multiple_of(lax.rem(z + lines - d, lines) * kd + grp * kp, kp), kp)]
        for e in range(1, n_groups):
            i = (d - 1) * (n_groups - 1) + e - 1
            c = remote(src, src, s_winx.at[i], r_winx.at[i], across(e))
            c.start()
            winx_sends.append(c)

    op = wide // n_groups
    mine = pl.ds(pl.multiple_of(grp * op, op), op)
    wo_sends = []
    for d in range(1, lines):
        c = remote(
            w_out.at[mine], wl.at[0, z, mine], s_wo.at[d - 1], r_wo.at[d - 1],
            at(lax.rem(z + d, lines) * QUAD + q),
        )
        c.start()
        wo_sends.append(c)
    y_peer = at(z * QUAD + lax.rem(q + half, QUAD))
    woy_sends = [remote(w_out.at[mine], wl.at[1, z, mine], s_woy.at[0], r_woy.at[0], y_peer)]

    loads[2].wait()
    expand(dnw, dns)

    loads[0].wait()
    for c in winx_sends:
        c.wait_recv()
    for c in tok_sends:
        c.wait_recv()

    part = jnp.dot(
        tr[...].reshape((QUAD - 1) * toks, lines * kd), win[...], preferred_element_type=F32
    ).astype(BF16)
    ps[...] = part.reshape(QUAD - 1, toks, wide)
    par_sends = []
    for d in range(1, QUAD):
        c = remote(
            ps.at[d - 1], pr.at[d - 1], s_par.at[d - 1], r_par.at[d - 1],
            at(z * QUAD + lax.rem(q + QUAD - d, QUAD)),
        )
        c.start()
        par_sends.append(c)
    total = jnp.dot(tq[q], win[...], preferred_element_type=F32)
    for d in range(1, QUAD):
        par_sends[d - 1].wait_recv()
        total = total + pr[d - 1].astype(F32)
    lat[...] = total.astype(BF16)

    disp[...] = lax.dot_general(
        hits[...], lat[...], (((0,), (0,)), ((), ())), preferred_element_type=F32
    ).astype(BF16)

    def block(i):
        return pl.ds(pl.multiple_of(i * cap, cap), cap)

    def dispatch(d):
        to = lax.rem(me + d, n)
        return remote(disp.at[block(to)], rows_in.at[block(d)], s_disp.at[d], r_disp.at[d], at(to))

    def give_back(d):
        to = lax.rem(me + n - d, n)
        return remote(res.at[block(d)], back.at[block(me)], s_ret.at[d], r_ret.at[d], at(to))

    for d in range(1, n):
        dispatch(d).start()
    rows_in[0:cap] = disp[block(me)]

    woy_sends[0].start()
    wox_sends = []

    def over_groups(ref):
        for e in range(1, n_groups):
            i = len(wox_sends)
            c = remote(ref, ref, s_wox.at[i], r_wox.at[i], across(e))
            c.start()
            wox_sends.append(c)

    for d in range(1, lines):
        wo_sends[d - 1].wait_recv()
        frm = lax.rem(z + lines - d, lines)
        c = remote(wl.at[0, frm, mine], wl.at[1, frm, mine], s_woy.at[d], r_woy.at[d], y_peer)
        c.start()
        woy_sends.append(c)
        over_groups(wl.at[0, frm, mine])

    def chunk(k, carry):
        for i in range(CHUNK):
            d = k * CHUNK + i

            @pl.when(d > 0)
            def _():
                dispatch(d).wait_recv()

        rows = pl.ds(pl.multiple_of(k * CHUNK * cap, CHUNK * cap), CHUNK * cap)
        hidden = jnp.dot(rows_in[rows], upw[...], preferred_element_type=F32)
        act[...] = jnp.square(jnp.maximum(hidden, 0.0)).astype(BF16)
        res[rows] = jnp.dot(act[...], dnw[...], preferred_element_type=F32).astype(BF16)
        for i in range(CHUNK):
            d = k * CHUNK + i

            @pl.when(d > 0)
            def _():
                give_back(d).start()

        return carry

    lax.fori_loop(0, n // CHUNK, chunk, 0)

    for d in range(lines):
        woy_sends[d].wait_recv()
        over_groups(wl.at[1, lax.rem(z + lines - d, lines), mine])

    back[block(me)] = res[0:cap]
    for d in range(1, n):
        give_back(d).wait_recv()
    combined = jnp.dot(ghi[...], back[...], preferred_element_type=F32) + jnp.dot(
        glo[...], back[...], preferred_element_type=F32
    )
    comb[0:toks] = combined.astype(BF16)
    pair = at(z * QUAD + q + 1 - 2 * lax.rem(q, 2))
    share = remote(comb.at[0:toks], comb.at[toks : 2 * toks], s_comb, r_comb, pair)
    share.start()
    loads[3].wait()
    for c in wox_sends:
        c.wait_recv()
    share.wait_recv()

    def columns(i):
        owner = lax.rem(i, lines) * QUAD + lax.rem(q + half * (i // lines), QUAD)
        return pl.ds(pl.multiple_of(owner * wd, wd), wd)

    def hand_over(i):
        return remote(sb.at[i], out_v.at[:, columns(i)], s_out.at[i], r_out.at[i], pair)

    def project(i, carry):
        both = jnp.dot(
            comb[...], wl[i // lines, lax.rem(i, lines)], preferred_element_type=F32
        ).astype(BF16)
        out_v[:, columns(i)] = both[0:toks]
        sb[i] = both[toks : 2 * toks]
        hand_over(i).start()
        return carry

    lax.fori_loop(0, 2 * lines, project, 0)
    for i in range(2 * lines):
        hand_over(i).wait_recv()
    final = pltpu.make_async_copy(out_v, out, s_local.at[4])
    final.start()
    for c in win_sends + winx_sends + tok_sends + par_sends + wo_sends + woy_sends + wox_sends + [share]:
        c.wait_send()
    for d in range(1, n):
        dispatch(d).wait_send()
        give_back(d).wait_send()
    for i in range(2 * lines):
        hand_over(i).wait_send()
    final.wait()


def kernel_body(
    n, n_groups,
    tokens, weight_in, weight_out, up_quant, up_scale, down_quant, down_scale, routing, gate_weights,
):
    toks, top = routing.shape
    cap = -(-capacity_of(toks, top, n) // 16) * 16
    lines = n // QUAD
    kd, wide = weight_in.shape
    wd = weight_out.shape[1]
    hid = up_quant.shape[2]
    slots = n * cap

    def vm(*shape):
        return pltpu.VMEM(shape, BF16)

    def sem(*shape):
        return pltpu.SemaphoreType.DMA(shape)

    others = n_groups - 1
    hbm = pl.BlockSpec(memory_space=pl.ANY)
    smem = pl.BlockSpec(memory_space=pltpu.SMEM)
    vmem = pl.BlockSpec(memory_space=pltpu.VMEM)
    flops = 2 * toks * kd * n * wide + 4 * slots * wide * hid + 2 * toks * wide * wd * n
    return pl.pallas_call(
        functools.partial(layer_kernel, n, n_groups, cap),
        out_shape=jax.ShapeDtypeStruct((toks, wd * n), BF16),
        in_specs=[hbm, hbm, hbm, hbm, smem, hbm, smem, vmem, vmem],
        out_specs=hbm,
        scratch_shapes=[
            vm(lines * kd, wide),
            vm(QUAD, toks, lines * kd),
            vm(QUAD - 1, toks, lines * kd),
            vm(QUAD - 1, toks, wide),
            vm(QUAD - 1, toks, wide),
            vm(toks, wide),
            vm(toks, slots),
            vm(toks, slots),
            vm(toks, slots),
            vm(slots, wide),
            vm(slots, wide),
            vm(slots, wide),
            vm(slots, wide),
            vm(wide, hid),
            vm(hid, wide),
            vm(CHUNK * cap, hid),
            vm(2, lines, wide, wd),
            vm(2 * toks, wide),
            vm(16, 128),
            vm(2 * lines, toks, wd),
            vm(toks, wd * n),
            sem(5), sem(n),
            sem(lines), sem(lines), sem(lines * others + 1), sem(lines * others + 1),
            sem(QUAD), sem(QUAD), sem(QUAD), sem(QUAD),
            sem(n), sem(n), sem(n), sem(n),
            sem(lines), sem(lines), sem(lines), sem(lines),
            sem(2 * lines * others + 1), sem(2 * lines * others + 1),
            pltpu.SemaphoreType.DMA, pltpu.SemaphoreType.DMA,
            sem(2 * lines), sem(2 * lines),
        ],
        compiler_params=pltpu.CompilerParams(
            collective_id=0, has_side_effects=True, vmem_limit_bytes=52 * 2**20
        ),
        cost_estimate=pl.CostEstimate(flops=flops, bytes_accessed=32 * 2**20, transcendentals=0),
    )(
        tokens, weight_in, weight_out,
        up_quant.reshape(wide, hid), up_scale.reshape(up_scale.shape[1:]),
        down_quant.reshape(hid, wide), down_scale.reshape(down_scale.shape[1:]),
        routing, gate_weights,
    )


def solution(mesh):
    n, n_groups = mesh.shape["col"], mesh.shape["groups"]

    def body(*args):
        tokens, weight_in, weight_out, up_quant = args[:4]
        fits = (
            n % QUAD == 0
            and (n // CHUNK) * CHUNK == n
            and up_quant.shape[0] == 1
            and weight_in.shape[0] % 128 == 0
            and weight_out.shape[1] % 128 == 0
        )
        if fits:
            return kernel_body(n, n_groups, *args)
        return plain_body(*args)

    return jax.shard_map(
        body,
        mesh=mesh,
        in_specs=(
            P(("groups", "col"), None),
            P("col", None),
            P(None, "col"),
            P("col", None, None),
            P("col", None, None),
            P("col", None, None),
            P("col", None, None),
            P(("groups", "col"), None),
            P(("groups", "col"), None),
        ),
        out_specs=P(("groups", "col"), None),
        check_vma=False,
    )
```

```python
import functools

import jax
import jax.numpy as jnp
from jax import lax
from jax.experimental import pallas as pl
from jax.experimental.pallas import tpu as pltpu
from jax.sharding import PartitionSpec as P

QUAD = 4
MESH = pl.DeviceIdType.MESH
F32, BF16 = jnp.float32, jnp.bfloat16


def dequant(quant, scale):
    block = quant.shape[1] // scale.shape[1]
    expanded = jnp.repeat(jnp.repeat(scale, block, axis=-2), block, axis=-1)
    return (quant.astype(F32) * expanded).astype(BF16)


def capacity_of(tok_rows, top_count, experts):
    return max(2, 3 * tok_rows * top_count // (2 * experts))


def plain_body(
    tokens, weight_in, weight_out, up_quant, up_scale, down_quant, down_scale, routing, gate_weights
):
    tok_rows, top_count = routing.shape
    exp_local = up_quant.shape[0]
    n_devices = lax.axis_size("col")
    experts = exp_local * n_devices
    capacity = capacity_of(tok_rows, top_count, experts)
    width = weight_in.shape[1]
    slots_all = experts * capacity
    latent = jnp.dot(
        tokens,
        lax.all_gather(weight_in, "col", axis=0, tiled=True),
        preferred_element_type=F32,
    ).astype(BF16)
    flat = routing.reshape(-1)
    onehot = (flat[:, None] == jnp.arange(experts, dtype=jnp.int32)[None, :]).astype(BF16)
    places = jnp.arange(flat.shape[0], dtype=jnp.int32)
    earlier = (places[:, None] > places[None, :]).astype(BF16)
    before = jnp.dot(earlier, onehot, preferred_element_type=F32)
    slot_rank = jnp.sum(before * onehot.astype(F32), axis=1).astype(jnp.int32)
    target = flat * capacity + slot_rank
    hits = (target[:, None] == jnp.arange(slots_all, dtype=jnp.int32)[None, :]).astype(BF16)
    hits = jnp.sum(hits.reshape(tok_rows, top_count, slots_all), axis=1)
    outgoing = jnp.einsum("tr,tl->rl", hits, latent, preferred_element_type=F32).astype(BF16)
    outgoing = outgoing.reshape(n_devices, exp_local, capacity, width)
    up_w = dequant(up_quant, up_scale)
    down_w = dequant(down_quant, down_scale)
    piece = lax.all_to_all(outgoing, "col", split_axis=0, concat_axis=0, tiled=True)
    sources, local_count, count, lanes = piece.shape
    rows = piece.transpose(1, 0, 2, 3).reshape(local_count, sources * count, lanes)
    hidden = jnp.einsum("erl,elh->erh", rows, up_w, preferred_element_type=F32)
    act = jnp.square(jax.nn.relu(hidden)).astype(BF16)
    result = jnp.einsum("erh,ehl->erl", act, down_w, preferred_element_type=F32).astype(BF16)
    computed = result.reshape(local_count, sources, count, lanes).transpose(1, 0, 2, 3)
    returned = lax.all_to_all(computed, "col", split_axis=0, concat_axis=0, tiled=True)
    back_rows = returned.reshape(slots_all, width)
    picked = back_rows[target].reshape(tok_rows, top_count, width).astype(F32)
    combined = jnp.sum(picked * gate_weights[:, :, None], axis=1).astype(BF16)
    mixed = jnp.dot(
        combined,
        lax.all_gather(weight_out, "col", axis=1, tiled=True),
        preferred_element_type=F32,
    )
    return mixed.astype(BF16)


def layer_kernel(
    n, n_groups, cap,
    tokens, w_in, w_out, upq, ups, dnq, dns, routing, gates,
    out,
    win, tq, tr, ps, pr, plan, lat, hits, ghi, glo, disp, rows_in, res, back, mine_part, parts, upw, dnw, act, wl, comb,
    sb, out_v,
    s_local, s_tq, s_win, r_win, s_winx, r_winx, s_tok, r_tok, s_par, r_par, s_plan, r_plan, s_lat, r_lat, s_sum, r_sum, s_disp, r_disp, s_ret, r_ret,
    s_wo, r_wo, s_woy, r_woy, s_wox, r_wox, s_comb, r_comb, s_out, r_out,
):
    lines = n // QUAD
    half = QUAD // 2
    toks = tokens.shape[0]
    kd, wide = w_in.shape
    wd = w_out.shape[1]
    hid = upw.shape[1]
    top = routing.shape[1]
    slots = n * cap
    me, grp = lax.axis_index("col"), lax.axis_index("groups")
    z, q = me // QUAD, lax.rem(me, QUAD)

    def at(col):
        return (grp, col)

    def across(step):
        return (lax.rem(grp + step, n_groups), me)

    def remote(src, dst, send, recv, to):
        return pltpu.make_async_remote_copy(
            src_ref=src, dst_ref=dst, send_sem=send, recv_sem=recv, device_id=to, device_id_type=MESH
        )

    tok_loads = []
    for i in range(n):
        line, lane = i // QUAD, i % QUAD
        tok_loads.append(
            pltpu.make_async_copy(
                tokens.at[:, pl.ds(i * kd, kd)], tq.at[lane, :, pl.ds(line * kd, kd)], s_tq.at[i]
            )
        )
    my_rows = pl.ds(pl.multiple_of(z * kd, kd), kd)
    loads = [
        pltpu.make_async_copy(w_in, win.at[my_rows], s_local.at[0]),
        pltpu.make_async_copy(upq, upw, s_local.at[1]),
        pltpu.make_async_copy(dnq, dnw, s_local.at[2]),
        pltpu.make_async_copy(w_out, wl.at[0, z], s_local.at[3]),
    ]
    for c in tok_loads:
        c.start()
    for c in loads:
        c.start()

    barrier = pltpu.get_barrier_semaphore()
    for d in range(1, n):
        pl.semaphore_signal(barrier, inc=1, device_id=at(lax.rem(me + d, n)), device_id_type=MESH)
    for d in range(1, n_groups):
        pl.semaphore_signal(barrier, inc=1, device_id=across(d), device_id_type=MESH)
    pl.semaphore_wait(barrier, n - 1 + n_groups - 1)

    kp = kd // n_groups
    def win_piece(owner):
        return win.at[pl.ds(pl.multiple_of(owner * kd + grp * kp, kp), kp)]

    def hop(way, j):
        owner = jnp.clip(z - way * j, 0, lines - 1)
        nxt = jnp.clip(z + way, 0, lines - 1)
        i = j if way > 0 else lines + j
        return remote(win_piece(owner), win_piece(owner), s_win.at[i], r_win.at[i], at(nxt * QUAD + q))

    def hop_over(way, j, e):
        owner = jnp.clip(z - way * (j + 1), 0, lines - 1)
        i = ((j if way > 0 else lines + j) * n_groups) + e
        return remote(win_piece(owner), win_piece(owner), s_winx.at[i], r_winx.at[i], across(e))

    def has(way, j):
        return (z - way * j >= 0) & (z - way * j < lines)

    loads[0].wait()
    for way in (1, -1):
        pl.when(has(way, -1))(hop(way, 0).start)
    for c in tok_loads:
        c.wait()
    tok_sends = []
    for d in range(1, QUAD):
        to = lax.rem(q + d, QUAD)
        c = remote(tq.at[to], tr.at[d - 1], s_tok.at[d - 1], r_tok.at[d - 1], at(z * QUAD + to))
        c.start()
        tok_sends.append(c)

    lane_e = lax.broadcasted_iota(jnp.int32, (toks, n), 1)
    mask = jnp.zeros((toks, n), F32)
    gate = jnp.zeros((toks, n), F32)
    for k in range(top):
        eq = (routing[:, k : k + 1] == lane_e).astype(F32)
        mask = mask + eq
        gate = gate + eq * gates[:, k : k + 1]
    earlier = (
        lax.broadcasted_iota(jnp.int32, (toks, toks), 0) > lax.broadcasted_iota(jnp.int32, (toks, toks), 1)
    ).astype(F32).astype(BF16)
    rank = jnp.dot(earlier, mask.astype(BF16), preferred_element_type=F32)
    out_of_range = -float(1 << slots.bit_length())
    rank = jnp.where(mask > 0.5, rank, out_of_range).astype(BF16)
    gate_hi = gate.astype(BF16)
    gate_lo = (gate - gate_hi.astype(F32)).astype(BF16)
    lanes = plan.shape[2]

    def placed(part, values):
        shift = (
            lax.broadcasted_iota(jnp.int32, (n, lanes), 0) + part * n
            == lax.broadcasted_iota(jnp.int32, (n, lanes), 1)
        )
        return jnp.dot(values, shift.astype(F32).astype(BF16), preferred_element_type=F32)

    plan[0] = (placed(0, rank) + placed(1, gate_hi) + placed(2, gate_lo)).astype(BF16)

    def along(s, src, dst, send, recv):
        return remote(src, dst, send, recv, at(lax.rem(z + s, lines) * QUAD + q))

    plan_sends = []
    for s in range(1, lines):
        c = along(s, plan.at[0], plan.at[s], s_plan.at[s], r_plan.at[s])
        c.start()
        plan_sends.append(c)

    def expand(weights, scales):
        rows_n, cols_n = scales.shape
        br, bc = weights.shape[0] // rows_n, weights.shape[1] // cols_n

        def step(i, carry):
            rows = pl.ds(pl.multiple_of(i * br, br), br)
            for j in range(cols_n):
                cols = slice(j * bc, (j + 1) * bc)
                weights[rows, cols] = (weights[rows, cols].astype(F32) * scales[i, j]).astype(BF16)
            return carry

        lax.fori_loop(0, rows_n, step, 0)

    for j in range(lines - 1):
        for way in (1, -1):
            @pl.when(has(way, j + 1))
            def _():
                hop(way, j).wait_recv()
                if j + 1 < lines - 1:
                    pl.when(has(way, -1))(hop(way, j + 1).start)
                for e in range(1, n_groups):
                    hop_over(way, j, e).start()

    op = wide // n_groups
    mine = pl.ds(pl.multiple_of(grp * op, op), op)
    wo_sends = []
    for d in range(1, lines):
        c = remote(
            w_out.at[mine], wl.at[0, z, mine], s_wo.at[d - 1], r_wo.at[d - 1],
            at(lax.rem(z + d, lines) * QUAD + q),
        )
        c.start()
        wo_sends.append(c)
    y_peer = at(z * QUAD + lax.rem(q + half, QUAD))
    woy_sends = [remote(w_out.at[mine], wl.at[1, z, mine], s_woy.at[0], r_woy.at[0], y_peer)]

    loads[1].wait()
    expand(upw, ups)
    loads[2].wait()
    expand(dnw, dns)

    for j in range(lines - 1):
        for way in (1, -1):
            @pl.when(has(way, j + 1))
            def _():
                for e in range(1, n_groups):
                    hop_over(way, j, e).wait_recv()

    qs = QUAD * cap
    row = lax.broadcasted_iota(jnp.int32, (lanes, qs), 0)
    col = lax.broadcasted_iota(jnp.int32, (lanes, qs), 1)

    def spread(part):
        expert = row - part * n - z * QUAD
        inside = (expert >= 0) & (expert < QUAD) & (col >= expert * cap) & (col < expert * cap + cap)
        return inside.astype(F32)

    first = spread(0)
    start = jnp.sum(first * ((row - z * QUAD) * cap).astype(F32), axis=0, keepdims=True)
    first, second, third = first.astype(BF16), spread(1).astype(BF16), spread(2).astype(BF16)
    slot = lax.broadcasted_iota(jnp.int32, (toks, qs), 1).astype(F32)
    for s in range(lines):
        if s > 0:
            plan_sends[s - 1].wait_recv()
        rank_x = jnp.dot(plan[s], first, preferred_element_type=F32)
        hit = (rank_x + start == slot).astype(F32)
        hits[s] = hit.astype(BF16)
        ghi[s] = (hit * jnp.dot(plan[s], second, preferred_element_type=F32)).astype(BF16)
        glo[s] = (hit * jnp.dot(plan[s], third, preferred_element_type=F32)).astype(BF16)

    for c in tok_sends:
        c.wait_recv()

    part = jnp.dot(
        tr[...].reshape((QUAD - 1) * toks, lines * kd), win[...], preferred_element_type=F32
    ).astype(BF16)
    ps[...] = part.reshape(QUAD - 1, toks, wide)
    par_sends = []
    for d in range(1, QUAD):
        c = remote(
            ps.at[d - 1], pr.at[d - 1], s_par.at[d - 1], r_par.at[d - 1],
            at(z * QUAD + lax.rem(q + QUAD - d, QUAD)),
        )
        c.start()
        par_sends.append(c)
    total = jnp.dot(tq[q], win[...], preferred_element_type=F32)
    for d in range(1, QUAD):
        par_sends[d - 1].wait_recv()
        total = total + pr[d - 1].astype(F32)
    lat[0] = total.astype(BF16)

    def lat_send(s):
        return along(s, lat.at[0], lat.at[s], s_lat.at[s], r_lat.at[s])

    for s in range(1, lines):
        lat_send(s).start()

    def block(i):
        return pl.ds(pl.multiple_of(i * cap, cap), cap)

    def dispatch(s, d):
        to, i = lax.rem(q + d, QUAD), s * QUAD + d
        return remote(
            disp.at[block(s * QUAD + to)], rows_in.at[block(i)], s_disp.at[i], r_disp.at[i], at(z * QUAD + to)
        )

    def give_back(s, d):
        to, i = lax.rem(q + QUAD - d, QUAD), s * QUAD + d
        return remote(
            res.at[block(i)], back.at[block(s * QUAD + q)], s_ret.at[i], r_ret.at[i], at(z * QUAD + to)
        )

    def share_send(s):
        to = lax.rem(z + lines - s, lines) * QUAD + q
        return remote(mine_part.at[s], parts.at[s], s_sum.at[s], r_sum.at[s], at(to))

    def rows_of(s):
        return pl.ds(pl.multiple_of(s * qs, qs), qs)

    def send_rows(s):
        disp[rows_of(s)] = lax.dot_general(
            hits[s], lat[s], (((0,), (0,)), ((), ())), preferred_element_type=F32
        ).astype(BF16)
        for d in range(1, QUAD):
            dispatch(s, d).start()
        rows_in[block(s * QUAD)] = disp[block(s * QUAD + q)]

    def collect(s):
        for d in range(1, QUAD):
            give_back(s, d).wait_recv()
        rows = back[rows_of(s)]
        mine_part[s] = (
            jnp.dot(ghi[s], rows, preferred_element_type=F32)
            + jnp.dot(glo[s], rows, preferred_element_type=F32)
        ).astype(BF16)
        pl.when(s > 0)(lambda: share_send(s).start())

    wox_sends = []

    def over_groups(ref):
        made = []
        for e in range(1, n_groups):
            i = len(wox_sends)
            c = remote(ref, ref, s_wox.at[i], r_wox.at[i], across(e))
            wox_sends.append(c)
            made.append(c)
        return made

    near, far = [], []
    for d in range(1, lines):
        frm = lax.rem(z + lines - d, lines)
        woy_sends.append(
            remote(wl.at[0, frm, mine], wl.at[1, frm, mine], s_woy.at[d], r_woy.at[d], y_peer)
        )
        near += over_groups(wl.at[0, frm, mine])
    for d in range(lines):
        far += over_groups(wl.at[1, lax.rem(z + lines - d, lines), mine])

    send_rows(0)

    def chunk(s, carry):
        @pl.when(s + 1 < lines)
        def _():
            lat_send(s + 1).wait_recv()
            send_rows(s + 1)

        for d in range(1, QUAD):
            dispatch(s, d).wait_recv()

        @pl.when(s == 1)
        def _():
            woy_sends[0].start()
            for c in wo_sends:
                c.wait_recv()
            for c in woy_sends[1:] + near:
                c.start()

        rows = rows_of(s)
        hidden = jnp.dot(rows_in[rows], upw[...], preferred_element_type=F32)
        act[...] = jnp.square(jnp.maximum(hidden, 0.0)).astype(BF16)
        res[rows] = jnp.dot(act[...], dnw[...], preferred_element_type=F32).astype(BF16)
        for d in range(1, QUAD):
            give_back(s, d).start()
        back[block(s * QUAD + q)] = res[block(s * QUAD)]
        pl.when(s > 0)(lambda: collect(s - 1))
        return carry

    lax.fori_loop(0, lines, chunk, 0)
    collect(lines - 1)

    for c in woy_sends:
        c.wait_recv()
    for c in far:
        c.start()
    combined = mine_part[0].astype(F32)
    for s in range(1, lines):
        share_send(s).wait_recv()
        combined = combined + parts[s].astype(F32)
    comb[0:toks] = combined.astype(BF16)
    pair = at(z * QUAD + q + 1 - 2 * lax.rem(q, 2))
    share = remote(comb.at[0:toks], comb.at[toks : 2 * toks], s_comb, r_comb, pair)
    share.start()
    loads[3].wait()
    for c in wox_sends:
        c.wait_recv()
    share.wait_recv()

    def columns(i):
        owner = lax.rem(i, lines) * QUAD + lax.rem(q + half * (i // lines), QUAD)
        return pl.ds(pl.multiple_of(owner * wd, wd), wd)

    def hand_over(i):
        return remote(sb.at[i], out_v.at[:, columns(i)], s_out.at[i], r_out.at[i], pair)

    def project(i, carry):
        both = jnp.dot(
            comb[...], wl[i // lines, lax.rem(i, lines)], preferred_element_type=F32
        ).astype(BF16)
        out_v[:, columns(i)] = both[0:toks]
        sb[i] = both[toks : 2 * toks]
        hand_over(i).start()
        return carry

    lax.fori_loop(0, 2 * lines, project, 0)
    for i in range(2 * lines):
        hand_over(i).wait_recv()
    final = pltpu.make_async_copy(out_v, out, s_local.at[4])
    final.start()
    for c in plan_sends + tok_sends + par_sends + wo_sends + woy_sends + wox_sends + [share]:
        c.wait_send()
    for j in range(lines - 1):
        for way in (1, -1):
            @pl.when(has(way, j) & has(way, -1))
            def _():
                hop(way, j).wait_send()

            @pl.when(has(way, j + 1))
            def _():
                for e in range(1, n_groups):
                    hop_over(way, j, e).wait_send()

    for s in range(lines):
        for d in range(1, QUAD):
            dispatch(s, d).wait_send()
            give_back(s, d).wait_send()
        if s > 0:
            lat_send(s).wait_send()
            share_send(s).wait_send()
    for i in range(2 * lines):
        hand_over(i).wait_send()
    final.wait()


def kernel_body(
    n, n_groups,
    tokens, weight_in, weight_out, up_quant, up_scale, down_quant, down_scale, routing, gate_weights,
):
    toks, top = routing.shape
    cap = -(-capacity_of(toks, top, n) // 16) * 16
    lines = n // QUAD
    kd, wide = weight_in.shape
    wd = weight_out.shape[1]
    hid = up_quant.shape[2]
    slots = n * cap

    def vm(*shape):
        return pltpu.VMEM(shape, BF16)

    def sem(*shape):
        return pltpu.SemaphoreType.DMA(shape)

    others = n_groups - 1
    hbm = pl.BlockSpec(memory_space=pl.ANY)
    smem = pl.BlockSpec(memory_space=pltpu.SMEM)
    vmem = pl.BlockSpec(memory_space=pltpu.VMEM)
    flops = 2 * toks * kd * n * wide + 4 * slots * wide * hid + 2 * toks * wide * wd * n
    return pl.pallas_call(
        functools.partial(layer_kernel, n, n_groups, cap),
        out_shape=jax.ShapeDtypeStruct((toks, wd * n), BF16),
        in_specs=[hbm, hbm, hbm, hbm, smem, hbm, smem, vmem, vmem],
        out_specs=hbm,
        scratch_shapes=[
            vm(lines * kd, wide),
            vm(QUAD, toks, lines * kd),
            vm(QUAD - 1, toks, lines * kd),
            vm(QUAD - 1, toks, wide),
            vm(QUAD - 1, toks, wide),
            vm(lines, toks, -(-3 * n // 128) * 128),
            vm(lines, toks, wide),
            vm(lines, toks, QUAD * cap),
            vm(lines, toks, QUAD * cap),
            vm(lines, toks, QUAD * cap),
            vm(slots, wide),
            vm(slots, wide),
            vm(slots, wide),
            vm(slots, wide),
            vm(lines, toks, wide),
            vm(lines, toks, wide),
            vm(wide, hid),
            vm(hid, wide),
            vm(QUAD * cap, hid),
            vm(2, lines, wide, wd),
            vm(2 * toks, wide),
            vm(2 * lines, toks, wd),
            vm(toks, wd * n),
            sem(5), sem(n),
            sem(2 * lines), sem(2 * lines), sem(2 * lines * n_groups), sem(2 * lines * n_groups),
            sem(QUAD), sem(QUAD), sem(QUAD), sem(QUAD),
            sem(lines), sem(lines), sem(lines), sem(lines), sem(lines), sem(lines),
            sem(n), sem(n), sem(n), sem(n),
            sem(lines), sem(lines), sem(lines), sem(lines),
            sem(2 * lines * others + 1), sem(2 * lines * others + 1),
            pltpu.SemaphoreType.DMA, pltpu.SemaphoreType.DMA,
            sem(2 * lines), sem(2 * lines),
        ],
        compiler_params=pltpu.CompilerParams(
            collective_id=0, has_side_effects=True, vmem_limit_bytes=52 * 2**20
        ),
        cost_estimate=pl.CostEstimate(flops=flops, bytes_accessed=32 * 2**20, transcendentals=0),
    )(
        tokens, weight_in, weight_out,
        up_quant.reshape(wide, hid), up_scale.reshape(up_scale.shape[1:]),
        down_quant.reshape(hid, wide), down_scale.reshape(down_scale.shape[1:]),
        routing, gate_weights,
    )


def solution(mesh):
    n, n_groups = mesh.shape["col"], mesh.shape["groups"]

    def body(*args):
        tokens, weight_in, weight_out, up_quant = args[:4]
        fits = (
            n % QUAD == 0
            and up_quant.shape[0] == 1
            and weight_in.shape[0] % 128 == 0
            and weight_out.shape[1] % 128 == 0
        )
        if fits:
            return kernel_body(n, n_groups, *args)
        return plain_body(*args)

    return jax.shard_map(
        body,
        mesh=mesh,
        in_specs=(
            P(("groups", "col"), None),
            P("col", None),
            P(None, "col"),
            P("col", None, None),
            P("col", None, None),
            P("col", None, None),
            P("col", None, None),
            P(("groups", "col"), None),
            P(("groups", "col"), None),
        ),
        out_specs=P(("groups", "col"), None),
        check_vma=False,
    )
```

```python
import functools

import jax
import jax.numpy as jnp
from jax import lax
from jax.experimental import pallas as pl
from jax.experimental.pallas import tpu as pltpu
from jax.sharding import PartitionSpec as P

QUAD = 4
MESH = pl.DeviceIdType.MESH
F32, BF16 = jnp.float32, jnp.bfloat16


def dequant(quant, scale):
    block = quant.shape[1] // scale.shape[1]
    expanded = jnp.repeat(jnp.repeat(scale, block, axis=-2), block, axis=-1)
    return (quant.astype(F32) * expanded).astype(BF16)


def capacity_of(tok_rows, top_count, experts):
    return max(2, 3 * tok_rows * top_count // (2 * experts))


def plain_body(
    tokens, weight_in, weight_out, up_quant, up_scale, down_quant, down_scale, routing, gate_weights
):
    tok_rows, top_count = routing.shape
    exp_local = up_quant.shape[0]
    n_devices = lax.axis_size("col")
    experts = exp_local * n_devices
    capacity = capacity_of(tok_rows, top_count, experts)
    width = weight_in.shape[1]
    slots_all = experts * capacity
    latent = jnp.dot(
        tokens,
        lax.all_gather(weight_in, "col", axis=0, tiled=True),
        preferred_element_type=F32,
    ).astype(BF16)
    flat = routing.reshape(-1)
    onehot = (flat[:, None] == jnp.arange(experts, dtype=jnp.int32)[None, :]).astype(BF16)
    places = jnp.arange(flat.shape[0], dtype=jnp.int32)
    earlier = (places[:, None] > places[None, :]).astype(BF16)
    before = jnp.dot(earlier, onehot, preferred_element_type=F32)
    slot_rank = jnp.sum(before * onehot.astype(F32), axis=1).astype(jnp.int32)
    target = flat * capacity + slot_rank
    hits = (target[:, None] == jnp.arange(slots_all, dtype=jnp.int32)[None, :]).astype(BF16)
    hits = jnp.sum(hits.reshape(tok_rows, top_count, slots_all), axis=1)
    outgoing = jnp.einsum("tr,tl->rl", hits, latent, preferred_element_type=F32).astype(BF16)
    outgoing = outgoing.reshape(n_devices, exp_local, capacity, width)
    up_w = dequant(up_quant, up_scale)
    down_w = dequant(down_quant, down_scale)
    piece = lax.all_to_all(outgoing, "col", split_axis=0, concat_axis=0, tiled=True)
    sources, local_count, count, lanes = piece.shape
    rows = piece.transpose(1, 0, 2, 3).reshape(local_count, sources * count, lanes)
    hidden = jnp.einsum("erl,elh->erh", rows, up_w, preferred_element_type=F32)
    act = jnp.square(jax.nn.relu(hidden)).astype(BF16)
    result = jnp.einsum("erh,ehl->erl", act, down_w, preferred_element_type=F32).astype(BF16)
    computed = result.reshape(local_count, sources, count, lanes).transpose(1, 0, 2, 3)
    returned = lax.all_to_all(computed, "col", split_axis=0, concat_axis=0, tiled=True)
    back_rows = returned.reshape(slots_all, width)
    picked = back_rows[target].reshape(tok_rows, top_count, width).astype(F32)
    combined = jnp.sum(picked * gate_weights[:, :, None], axis=1).astype(BF16)
    mixed = jnp.dot(
        combined,
        lax.all_gather(weight_out, "col", axis=1, tiled=True),
        preferred_element_type=F32,
    )
    return mixed.astype(BF16)


def layer_kernel(
    n, n_groups, cap,
    tokens, w_in, w_out, upq, ups, dnq, dns, routing, gates,
    out,
    win, tq, tr, ps, pr, plan, lat, hits, ghi, glo, disp, rows_in, res, back, mine_part, parts, upw, dnw, act, wl, comb,
    sb, out_v,
    s_local, s_tq, s_win, r_win, s_winx, r_winx, s_tok, r_tok, s_par, r_par, s_plan, r_plan, s_lat, r_lat, s_sum, r_sum, s_disp, r_disp, s_ret, r_ret,
    s_wo, r_wo, s_woy, r_woy, s_wox, r_wox, s_comb, r_comb, s_out, r_out,
):
    lines = n // QUAD
    half = QUAD // 2
    toks = tokens.shape[0]
    kd, wide = w_in.shape
    wd = w_out.shape[1]
    hid = upw.shape[1]
    top = routing.shape[1]
    slots = n * cap
    me, grp = lax.axis_index("col"), lax.axis_index("groups")
    z, q = me // QUAD, lax.rem(me, QUAD)

    def at(col):
        return (grp, col)

    def across(step):
        return (lax.rem(grp + step, n_groups), me)

    def remote(src, dst, send, recv, to):
        return pltpu.make_async_remote_copy(
            src_ref=src, dst_ref=dst, send_sem=send, recv_sem=recv, device_id=to, device_id_type=MESH
        )

    tok_loads = []
    for i in range(n):
        line, lane = i // QUAD, i % QUAD
        tok_loads.append(
            pltpu.make_async_copy(
                tokens.at[:, pl.ds(i * kd, kd)], tq.at[lane, :, pl.ds(line * kd, kd)], s_tq.at[i]
            )
        )
    my_rows = pl.ds(pl.multiple_of(z * kd, kd), kd)
    loads = [
        pltpu.make_async_copy(w_in, win.at[my_rows], s_local.at[0]),
        pltpu.make_async_copy(upq, upw, s_local.at[1]),
        pltpu.make_async_copy(dnq, dnw, s_local.at[2]),
        pltpu.make_async_copy(w_out, wl.at[0, z], s_local.at[3]),
    ]
    for c in tok_loads:
        c.start()
    for c in loads:
        c.start()

    barrier = pltpu.get_barrier_semaphore()
    for d in range(1, n):
        pl.semaphore_signal(barrier, inc=1, device_id=at(lax.rem(me + d, n)), device_id_type=MESH)
    for d in range(1, n_groups):
        pl.semaphore_signal(barrier, inc=1, device_id=across(d), device_id_type=MESH)
    pl.semaphore_wait(barrier, n - 1 + n_groups - 1)

    kp = kd // n_groups
    def win_piece(owner):
        return win.at[pl.ds(pl.multiple_of(owner * kd + grp * kp, kp), kp)]

    def hop(way, j):
        owner = jnp.clip(z - way * j, 0, lines - 1)
        nxt = jnp.clip(z + way, 0, lines - 1)
        i = j if way > 0 else lines + j
        return remote(win_piece(owner), win_piece(owner), s_win.at[i], r_win.at[i], at(nxt * QUAD + q))

    def hop_over(way, j, e):
        owner = jnp.clip(z - way * (j + 1), 0, lines - 1)
        i = ((j if way > 0 else lines + j) * n_groups) + e
        return remote(win_piece(owner), win_piece(owner), s_winx.at[i], r_winx.at[i], across(e))

    def has(way, j):
        return (z - way * j >= 0) & (z - way * j < lines)

    loads[0].wait()
    for way in (1, -1):
        pl.when(has(way, -1))(hop(way, 0).start)
    for c in tok_loads:
        c.wait()
    tok_sends = []
    for d in range(1, QUAD):
        to = lax.rem(q + d, QUAD)
        c = remote(tq.at[to], tr.at[d - 1], s_tok.at[d - 1], r_tok.at[d - 1], at(z * QUAD + to))
        c.start()
        tok_sends.append(c)

    lane_e = lax.broadcasted_iota(jnp.int32, (toks, n), 1)
    mask = jnp.zeros((toks, n), F32)
    gate = jnp.zeros((toks, n), F32)
    for k in range(top):
        eq = (routing[:, k : k + 1] == lane_e).astype(F32)
        mask = mask + eq
        gate = gate + eq * gates[:, k : k + 1]
    earlier = (
        lax.broadcasted_iota(jnp.int32, (toks, toks), 0) > lax.broadcasted_iota(jnp.int32, (toks, toks), 1)
    ).astype(F32).astype(BF16)
    rank = jnp.dot(earlier, mask.astype(BF16), preferred_element_type=F32)
    out_of_range = -float(1 << slots.bit_length())
    rank = jnp.where(mask > 0.5, rank, out_of_range).astype(BF16)
    gate_hi = gate.astype(BF16)
    gate_lo = (gate - gate_hi.astype(F32)).astype(BF16)
    lanes = plan.shape[2]

    def placed(part, values):
        shift = (
            lax.broadcasted_iota(jnp.int32, (n, lanes), 0) + part * n
            == lax.broadcasted_iota(jnp.int32, (n, lanes), 1)
        )
        return jnp.dot(values, shift.astype(F32).astype(BF16), preferred_element_type=F32)

    plan[0] = (placed(0, rank) + placed(1, gate_hi) + placed(2, gate_lo)).astype(BF16)

    def along(s, src, dst, send, recv):
        return remote(src, dst, send, recv, at(lax.rem(z + s, lines) * QUAD + q))

    plan_sends = []
    for s in range(1, lines):
        c = along(s, plan.at[0], plan.at[s], s_plan.at[s], r_plan.at[s])
        c.start()
        plan_sends.append(c)

    def expand(weights, scales):
        rows_n, cols_n = scales.shape
        br, bc = weights.shape[0] // rows_n, weights.shape[1] // cols_n

        def step(i, carry):
            rows = pl.ds(pl.multiple_of(i * br, br), br)
            for j in range(cols_n):
                cols = slice(j * bc, (j + 1) * bc)
                weights[rows, cols] = (weights[rows, cols].astype(F32) * scales[i, j]).astype(BF16)
            return carry

        lax.fori_loop(0, rows_n, step, 0)

    for j in range(lines - 1):
        for way in (1, -1):
            @pl.when(has(way, j + 1))
            def _():
                hop(way, j).wait_recv()
                if j + 1 < lines - 1:
                    pl.when(has(way, -1))(hop(way, j + 1).start)
                for e in range(1, n_groups):
                    hop_over(way, j, e).start()

    op = wide // n_groups
    mine = pl.ds(pl.multiple_of(grp * op, op), op)
    wo_sends = []
    for d in range(1, lines):
        c = remote(
            w_out.at[mine], wl.at[0, z, mine], s_wo.at[d - 1], r_wo.at[d - 1],
            at(lax.rem(z + d, lines) * QUAD + q),
        )
        c.start()
        wo_sends.append(c)
    y_peer = at(z * QUAD + lax.rem(q + half, QUAD))
    woy_sends = [remote(w_out.at[mine], wl.at[1, z, mine], s_woy.at[0], r_woy.at[0], y_peer)]
    woy_sends[0].start()

    loads[1].wait()
    expand(upw, ups)
    loads[2].wait()
    expand(dnw, dns)

    for j in range(lines - 1):
        for way in (1, -1):
            @pl.when(has(way, j + 1))
            def _():
                for e in range(1, n_groups):
                    hop_over(way, j, e).wait_recv()

    qs = QUAD * cap
    row = lax.broadcasted_iota(jnp.int32, (lanes, qs), 0)
    col = lax.broadcasted_iota(jnp.int32, (lanes, qs), 1)

    def spread(part):
        expert = row - part * n - z * QUAD
        inside = (expert >= 0) & (expert < QUAD) & (col >= expert * cap) & (col < expert * cap + cap)
        return inside.astype(F32)

    first = spread(0)
    start = jnp.sum(first * ((row - z * QUAD) * cap).astype(F32), axis=0, keepdims=True)
    first, second, third = first.astype(BF16), spread(1).astype(BF16), spread(2).astype(BF16)
    slot = lax.broadcasted_iota(jnp.int32, (toks, qs), 1).astype(F32)
    for s in range(lines):
        if s > 0:
            plan_sends[s - 1].wait_recv()
        rank_x = jnp.dot(plan[s], first, preferred_element_type=F32)
        hit = (rank_x + start == slot).astype(F32)
        hits[s] = hit.astype(BF16)
        ghi[s] = (hit * jnp.dot(plan[s], second, preferred_element_type=F32)).astype(BF16)
        glo[s] = (hit * jnp.dot(plan[s], third, preferred_element_type=F32)).astype(BF16)

    for c in tok_sends:
        c.wait_recv()

    part = jnp.dot(
        tr[...].reshape((QUAD - 1) * toks, lines * kd), win[...], preferred_element_type=F32
    ).astype(BF16)
    ps[...] = part.reshape(QUAD - 1, toks, wide)
    par_sends = []
    for d in range(1, QUAD):
        c = remote(
            ps.at[d - 1], pr.at[d - 1], s_par.at[d - 1], r_par.at[d - 1],
            at(z * QUAD + lax.rem(q + QUAD - d, QUAD)),
        )
        c.start()
        par_sends.append(c)
    total = jnp.dot(tq[q], win[...], preferred_element_type=F32)
    for d in range(1, QUAD):
        par_sends[d - 1].wait_recv()
        total = total + pr[d - 1].astype(F32)
    lat[0] = total.astype(BF16)

    def lat_send(s):
        return along(s, lat.at[0], lat.at[s], s_lat.at[s], r_lat.at[s])

    for s in range(1, lines):
        lat_send(s).start()

    def block(i):
        return pl.ds(pl.multiple_of(i * cap, cap), cap)

    def dispatch(s, d):
        to, i = lax.rem(q + d, QUAD), s * QUAD + d
        return remote(
            disp.at[block(s * QUAD + to)], rows_in.at[block(i)], s_disp.at[i], r_disp.at[i], at(z * QUAD + to)
        )

    def give_back(s, d):
        to, i = lax.rem(q + QUAD - d, QUAD), s * QUAD + d
        return remote(
            res.at[block(i)], back.at[block(s * QUAD + q)], s_ret.at[i], r_ret.at[i], at(z * QUAD + to)
        )

    def share_send(s):
        to = lax.rem(z + lines - s, lines) * QUAD + q
        return remote(mine_part.at[s], parts.at[s], s_sum.at[s], r_sum.at[s], at(to))

    def rows_of(s):
        return pl.ds(pl.multiple_of(s * qs, qs), qs)

    def send_rows(s):
        disp[rows_of(s)] = lax.dot_general(
            hits[s], lat[s], (((0,), (0,)), ((), ())), preferred_element_type=F32
        ).astype(BF16)
        for d in range(1, QUAD):
            dispatch(s, d).start()
        rows_in[block(s * QUAD)] = disp[block(s * QUAD + q)]

    def collect(s):
        for d in range(1, QUAD):
            give_back(s, d).wait_recv()
        rows = back[rows_of(s)]
        mine_part[s] = (
            jnp.dot(ghi[s], rows, preferred_element_type=F32)
            + jnp.dot(glo[s], rows, preferred_element_type=F32)
        ).astype(BF16)
        pl.when(s > 0)(lambda: share_send(s).start())

    wox_sends = []

    def over_groups(ref):
        made = []
        for e in range(1, n_groups):
            i = len(wox_sends)
            c = remote(ref, ref, s_wox.at[i], r_wox.at[i], across(e))
            wox_sends.append(c)
            made.append(c)
        return made

    near, far = [], []
    for d in range(1, lines):
        frm = lax.rem(z + lines - d, lines)
        woy_sends.append(
            remote(wl.at[0, frm, mine], wl.at[1, frm, mine], s_woy.at[d], r_woy.at[d], y_peer)
        )
        near.append(over_groups(wl.at[0, frm, mine]))
    for d in range(lines):
        far.append(over_groups(wl.at[1, lax.rem(z + lines - d, lines), mine]))

    send_rows(0)
    for d in range(1, lines):
        wo_sends[d - 1].wait_recv()
        for c in [woy_sends[d]] + near[d - 1]:
            c.start()

    def chunk(s, carry):
        @pl.when(s + 1 < lines)
        def _():
            lat_send(s + 1).wait_recv()
            send_rows(s + 1)

        for d in range(1, QUAD):
            dispatch(s, d).wait_recv()

        @pl.when(s == max(lines - 2, 0))
        def _():
            for d in range(lines):
                woy_sends[d].wait_recv()
                for c in far[d]:
                    c.start()

        rows = rows_of(s)
        hidden = jnp.dot(rows_in[rows], upw[...], preferred_element_type=F32)
        act[...] = jnp.square(jnp.maximum(hidden, 0.0)).astype(BF16)
        res[rows] = jnp.dot(act[...], dnw[...], preferred_element_type=F32).astype(BF16)
        for d in range(1, QUAD):
            give_back(s, d).start()
        back[block(s * QUAD + q)] = res[block(s * QUAD)]
        pl.when(s > 0)(lambda: collect(s - 1))
        return carry

    lax.fori_loop(0, lines, chunk, 0)
    collect(lines - 1)

    combined = mine_part[0].astype(F32)
    for s in range(1, lines):
        share_send(s).wait_recv()
        combined = combined + parts[s].astype(F32)
    comb[0:toks] = combined.astype(BF16)
    pair = at(z * QUAD + q + 1 - 2 * lax.rem(q, 2))
    share = remote(comb.at[0:toks], comb.at[toks : 2 * toks], s_comb, r_comb, pair)
    share.start()
    loads[3].wait()
    for c in wox_sends:
        c.wait_recv()
    share.wait_recv()

    def columns(i):
        owner = lax.rem(i, lines) * QUAD + lax.rem(q + half * (i // lines), QUAD)
        return pl.ds(pl.multiple_of(owner * wd, wd), wd)

    def hand_over(i):
        return remote(sb.at[i], out_v.at[:, columns(i)], s_out.at[i], r_out.at[i], pair)

    def project(i, carry):
        both = jnp.dot(
            comb[...], wl[i // lines, lax.rem(i, lines)], preferred_element_type=F32
        ).astype(BF16)
        out_v[:, columns(i)] = both[0:toks]
        sb[i] = both[toks : 2 * toks]
        hand_over(i).start()
        return carry

    lax.fori_loop(0, 2 * lines, project, 0)
    for i in range(2 * lines):
        hand_over(i).wait_recv()
    final = pltpu.make_async_copy(out_v, out, s_local.at[4])
    final.start()
    for c in plan_sends + tok_sends + par_sends + wo_sends + woy_sends + wox_sends + [share]:
        c.wait_send()
    for j in range(lines - 1):
        for way in (1, -1):
            @pl.when(has(way, j) & has(way, -1))
            def _():
                hop(way, j).wait_send()

            @pl.when(has(way, j + 1))
            def _():
                for e in range(1, n_groups):
                    hop_over(way, j, e).wait_send()

    for s in range(lines):
        for d in range(1, QUAD):
            dispatch(s, d).wait_send()
            give_back(s, d).wait_send()
        if s > 0:
            lat_send(s).wait_send()
            share_send(s).wait_send()
    for i in range(2 * lines):
        hand_over(i).wait_send()
    final.wait()


def kernel_body(
    n, n_groups,
    tokens, weight_in, weight_out, up_quant, up_scale, down_quant, down_scale, routing, gate_weights,
):
    toks, top = routing.shape
    cap = -(-capacity_of(toks, top, n) // 16) * 16
    lines = n // QUAD
    kd, wide = weight_in.shape
    wd = weight_out.shape[1]
    hid = up_quant.shape[2]
    slots = n * cap

    def vm(*shape):
        return pltpu.VMEM(shape, BF16)

    def sem(*shape):
        return pltpu.SemaphoreType.DMA(shape)

    others = n_groups - 1
    hbm = pl.BlockSpec(memory_space=pl.ANY)
    smem = pl.BlockSpec(memory_space=pltpu.SMEM)
    vmem = pl.BlockSpec(memory_space=pltpu.VMEM)
    flops = 2 * toks * kd * n * wide + 4 * slots * wide * hid + 2 * toks * wide * wd * n
    return pl.pallas_call(
        functools.partial(layer_kernel, n, n_groups, cap),
        out_shape=jax.ShapeDtypeStruct((toks, wd * n), BF16),
        in_specs=[hbm, hbm, hbm, hbm, smem, hbm, smem, vmem, vmem],
        out_specs=hbm,
        scratch_shapes=[
            vm(lines * kd, wide),
            vm(QUAD, toks, lines * kd),
            vm(QUAD - 1, toks, lines * kd),
            vm(QUAD - 1, toks, wide),
            vm(QUAD - 1, toks, wide),
            vm(lines, toks, -(-3 * n // 128) * 128),
            vm(lines, toks, wide),
            vm(lines, toks, QUAD * cap),
            vm(lines, toks, QUAD * cap),
            vm(lines, toks, QUAD * cap),
            vm(slots, wide),
            vm(slots, wide),
            vm(slots, wide),
            vm(slots, wide),
            vm(lines, toks, wide),
            vm(lines, toks, wide),
            vm(wide, hid),
            vm(hid, wide),
            vm(QUAD * cap, hid),
            vm(2, lines, wide, wd),
            vm(2 * toks, wide),
            vm(2 * lines, toks, wd),
            vm(toks, wd * n),
            sem(5), sem(n),
            sem(2 * lines), sem(2 * lines), sem(2 * lines * n_groups), sem(2 * lines * n_groups),
            sem(QUAD), sem(QUAD), sem(QUAD), sem(QUAD),
            sem(lines), sem(lines), sem(lines), sem(lines), sem(lines), sem(lines),
            sem(n), sem(n), sem(n), sem(n),
            sem(lines), sem(lines), sem(lines), sem(lines),
            sem(2 * lines * others + 1), sem(2 * lines * others + 1),
            pltpu.SemaphoreType.DMA, pltpu.SemaphoreType.DMA,
            sem(2 * lines), sem(2 * lines),
        ],
        compiler_params=pltpu.CompilerParams(
            collective_id=0, has_side_effects=True, vmem_limit_bytes=52 * 2**20
        ),
        cost_estimate=pl.CostEstimate(flops=flops, bytes_accessed=32 * 2**20, transcendentals=0),
    )(
        tokens, weight_in, weight_out,
        up_quant.reshape(wide, hid), up_scale.reshape(up_scale.shape[1:]),
        down_quant.reshape(hid, wide), down_scale.reshape(down_scale.shape[1:]),
        routing, gate_weights,
    )


def solution(mesh):
    n, n_groups = mesh.shape["col"], mesh.shape["groups"]

    def body(*args):
        tokens, weight_in, weight_out, up_quant = args[:4]
        fits = (
            n % QUAD == 0
            and up_quant.shape[0] == 1
            and weight_in.shape[0] % 128 == 0
            and weight_out.shape[1] % 128 == 0
        )
        if fits:
            return kernel_body(n, n_groups, *args)
        return plain_body(*args)

    return jax.shard_map(
        body,
        mesh=mesh,
        in_specs=(
            P(("groups", "col"), None),
            P("col", None),
            P(None, "col"),
            P("col", None, None),
            P("col", None, None),
            P("col", None, None),
            P("col", None, None),
            P(("groups", "col"), None),
            P(("groups", "col"), None),
        ),
        out_specs=P(("groups", "col"), None),
        check_vma=False,
    )
```
